256 devices in a mesh: rep: 4 (over y), fsdp: 64 (over z, x, core).
Axes of the slice: x: 4, y: 4, z: 8, core: 2. Of those that a mesh axis runs over, the one named last changes fastest.
Arguments:
- grads: bfloat16 [4, 16, 512, 8192], P('rep', None, 'fsdp'), may hold values from -5.4 to 5.4
- left_stat: float32 [4, 64, 2, 512, 512], P('rep', 'fsdp'), may hold values from -0.4 to 4.4
- right_stat: float32 [4, 64, 2, 512, 512], P('rep', 'fsdp'), may hold values from -0.4 to 4.4
- left_root: bfloat16 [4, 64, 2, 512, 512], P('rep', 'fsdp'), may hold values from -0.16 to 1.66
- right_root: bfloat16 [4, 64, 2, 512, 512], P('rep', 'fsdp'), may hold values from -0.16 to 1.66
- slot_block: int32 [4, 64, 2], replicated, may hold values from -1 to 63, as said below
Outputs:
- new_left: float32 [4, 64, 2, 512, 512], P('rep', 'fsdp')
- new_right: float32 [4, 64, 2, 512, 512], P('rep', 'fsdp')
- update: bfloat16 [16, 512, 8192], P('rep', 'fsdp')
The draws below stay inside these ranges and needn't reach their ends.
Inputs may be any that keep to these rules, and one draw needn't show every extreme that they name: `slot_block`: in every band each block number 0 to 63 stands in exactly one slot; an owner's used slots come first and -1 marks the rest; in every band some owner uses all 2 slots.
All inputs are finite; a program needn't handle non-finite values.
Results may differ from the reference program's by a relative error of at most 0.015.
Values may be sent and summed in bfloat16 or wider, within the bound.
No kernel may reach another device: no remote copies, remote signals or barrier semaphores. Data moves between devices by JAX's collectives and lax.ppermute only.
A program may use at most 64 MiB of HBM per device.

```python
import math
import jax
import jax.numpy as jnp
from jax import lax

D = 8192
BLOCK = 512
BAND_BR = 4
COL_BLOCKS = 16
BLOCKS_BAND = 64
SLOTS = 2
BLOCK_ROWS = 16
N_REP = 4
N_FSDP = 64


def symmetric_draw(key, diag_low, diag_high, off_scale):
    diag_key, noise_key = jax.random.split(key, 2)
    shape_full = (N_REP, N_FSDP, SLOTS, BLOCK, BLOCK)
    random_noise = jnp.clip(jax.random.normal(noise_key, shape_full, jnp.float32), -4.0, 4.0)
    paired = 0.5 * (random_noise + jnp.swapaxes(random_noise, 3, 4)) * off_scale
    diagonal = jax.random.uniform(diag_key, (N_REP, N_FSDP, SLOTS, BLOCK, 1), jnp.float32, diag_low, diag_high)
    identity_mask = (jnp.arange(BLOCK)[:, None] == jnp.arange(BLOCK)[None, :]).astype(jnp.float32)
    return paired + identity_mask * diagonal


def draw_grads(key, part):
    key = jax.random.fold_in(key, 1)
    row_key, col_key, noise_key = jax.random.split(key, 3)
    row_count = BLOCK_ROWS * BLOCK
    row_scale = jnp.exp(jax.random.uniform(row_key, (row_count,), jnp.float32, math.log(0.3), math.log(3.0)))
    col_scale = jnp.exp(jax.random.uniform(col_key, (D,), jnp.float32, math.log(0.3), math.log(3.0)))
    random_noise = jnp.clip(jax.random.normal(noise_key, (N_REP, row_count, D), jnp.float32), -5.0, 5.0)
    values = 0.12 * random_noise * row_scale[None, :, None] * col_scale[None, None, :]
    return values.reshape(N_REP, BLOCK_ROWS, BLOCK, D).astype(jnp.bfloat16)


def draw_left_stat(key, part):
    key = jax.random.fold_in(key, 2)
    return symmetric_draw(key, 1.0, 4.0, 0.1)


def draw_right_stat(key, part):
    key = jax.random.fold_in(key, 3)
    return symmetric_draw(key, 1.0, 4.0, 0.1)


def draw_left_root(key, part):
    key = jax.random.fold_in(key, 4)
    return symmetric_draw(key, 0.5, 1.5, 0.04).astype(jnp.bfloat16)


def draw_right_root(key, part):
    key = jax.random.fold_in(key, 5)
    return symmetric_draw(key, 0.5, 1.5, 0.04).astype(jnp.bfloat16)


def draw_slot_block(key, part):
    key = jax.random.fold_in(key, 6)

    def one_band(band_key):
        pair_key, fill_key, perm_key = jax.random.split(band_key, 3)
        owner_order = jax.random.permutation(pair_key, N_FSDP)
        first_half = jax.random.randint(fill_key, (N_FSDP // 2,), 0, SLOTS + 1)
        first_half = first_half.at[0].set(SLOTS)
        counts_paired = jnp.concatenate([first_half, SLOTS - first_half]).astype(jnp.int32)
        counts = jnp.zeros((N_FSDP,), jnp.int32).at[owner_order].set(counts_paired)
        starts = jnp.cumsum(counts) - counts
        blocks = jax.random.permutation(perm_key, BLOCKS_BAND).astype(jnp.int32)
        slot_ids = jnp.arange(SLOTS, dtype=jnp.int32)
        position = jnp.minimum(starts[:, None] + slot_ids[None, :], BLOCKS_BAND - 1)
        return jnp.where(slot_ids[None, :] < counts[:, None], blocks[position], -1).astype(jnp.int32)
    band_keys = jax.random.split(key, N_REP)
    return jax.vmap(one_band)(band_keys)


def setup_inputs(seed: int = 0) -> dict:
    streams_of = jax.random.split(jax.random.key(seed), 7)
    grads = draw_grads(jax.random.fold_in(streams_of[6], 71), 0)
    left_stat = draw_left_stat(jax.random.fold_in(streams_of[6], 71), 0)
    right_stat = draw_right_stat(jax.random.fold_in(streams_of[6], 71), 0)
    left_root = draw_left_root(jax.random.fold_in(streams_of[6], 71), 0)
    right_root = draw_right_root(jax.random.fold_in(streams_of[6], 71), 0)
    slot_block = draw_slot_block(jax.random.fold_in(streams_of[6], 71), 0)
    return {"grads": grads, "left_stat": left_stat, "right_stat": right_stat, "left_root": left_root, "right_root": right_root, "slot_block": slot_block}


beta_two = 0.95
epsilon = 1e-06
highest = lax.Precision.HIGHEST

def precondition(one_tile, left_prev, right_prev, left_inv, right_inv):
    gram_rows = lax.dot_general(one_tile, one_tile, (((1,), (1,)), ((), ())), precision=highest, preferred_element_type=jnp.float32)
    gram_cols = lax.dot_general(one_tile, one_tile, (((0,), (0,)), ((), ())), precision=highest, preferred_element_type=jnp.float32)
    new_left = beta_two * left_prev + (1.0 - beta_two) * gram_rows
    new_right = beta_two * right_prev + (1.0 - beta_two) * gram_cols
    shaped = jnp.dot(left_inv.astype(jnp.float32), one_tile, precision=highest, preferred_element_type=jnp.float32)
    shaped = jnp.dot(shaped, right_inv.astype(jnp.float32), precision=highest, preferred_element_type=jnp.float32)
    graft_ratio = jnp.sqrt(jnp.sum(one_tile * one_tile) / (jnp.sum(shaped * shaped) + epsilon))
    return (new_left, new_right, (shaped * graft_ratio).astype(jnp.bfloat16))

def reference(grads, left_stat, right_stat, left_root, right_root, slot_block):
    summed = lax.optimization_barrier(jnp.sum(grads.astype(jnp.float32), axis=0)).astype(jnp.bfloat16)
    blocks = summed.reshape(N_REP, BAND_BR, BLOCK, COL_BLOCKS, BLOCK).transpose(0, 1, 3, 2, 4).reshape(N_REP, BLOCKS_BAND, BLOCK, BLOCK)
    positions = jnp.arange(N_FSDP * SLOTS, dtype=jnp.int32)
    numbers = jnp.arange(BLOCKS_BAND, dtype=jnp.int32)
    left_list, right_list, pieces = ([], [], [])
    for band_index in range(N_REP):
        band_tiles = blocks[band_index]
        band_table = slot_block[band_index].reshape(N_FSDP * SLOTS)

        def one_slot(inputs):
            block_id, left_prev, right_prev, left_inv, right_inv = inputs
            one_tile = lax.dynamic_index_in_dim(band_tiles, jnp.maximum(block_id, 0), 0, keepdims=False).astype(jnp.float32)
            one_tile = jnp.where(block_id >= 0, one_tile, jnp.zeros_like(one_tile))
            return precondition(one_tile, left_prev, right_prev, left_inv, right_inv)
        new_left, new_right, scaled = lax.map(one_slot, (band_table, left_stat[band_index].reshape(N_FSDP * SLOTS, BLOCK, BLOCK), right_stat[band_index].reshape(N_FSDP * SLOTS, BLOCK, BLOCK), left_root[band_index].reshape(N_FSDP * SLOTS, BLOCK, BLOCK), right_root[band_index].reshape(N_FSDP * SLOTS, BLOCK, BLOCK)))
        locate = lax.optimization_barrier(jnp.sum(jnp.where(band_table[None, :] == numbers[:, None], positions[None, :], 0), axis=1, dtype=jnp.int32))
        placed = jnp.take(scaled, locate, axis=0)
        pieces.append(placed.reshape(BAND_BR, COL_BLOCKS, BLOCK, BLOCK).transpose(0, 2, 1, 3).reshape(BAND_BR, BLOCK, D))
        left_list.append(new_left.reshape(N_FSDP, SLOTS, BLOCK, BLOCK))
        right_list.append(new_right.reshape(N_FSDP, SLOTS, BLOCK, BLOCK))
    return (jnp.stack(left_list), jnp.stack(right_list), jnp.concatenate(pieces, axis=0))
```

```python
import jax
import jax.numpy as jnp
from jax import lax
from jax.experimental import pallas as pl
from jax.experimental.pallas import tpu as pltpu
from jax.sharding import PartitionSpec as P

beta_two = 0.95
epsilon = 1e-06
f32 = jnp.float32
bf16 = jnp.bfloat16
vmem_bytes = 48 * 1024 * 1024


def sum_and_pick(band_ref, table_ref, own_ref, left_ref, right_ref, out_ref, strips):
    band_rows, strip_rows, width = own_ref.shape
    order = strips.shape[2]
    col_blocks = width // order
    blocks = band_rows * col_blocks
    for row in range(band_rows):
        total = (
            own_ref[row].astype(f32) + left_ref[row].astype(f32) + right_ref[row].astype(f32)
        ).astype(bf16)
        for col in range(col_blocks):
            strips[row * col_blocks + col] = total[:, col * order : (col + 1) * order]
    strips[blocks] = jnp.zeros((strip_rows, order), bf16)
    owners, slots = out_ref.shape[:2]

    def body(owner, carry):
        for slot in range(slots):
            block = table_ref[owner * slots + slot]
            out_ref[owner, slot] = strips[jnp.where(block >= 0, block, blocks)]
        return carry

    lax.fori_loop(0, owners, body, 0, unroll=4)


def shape_tiles(tile_ref, left_ref, right_ref, out_ref):
    owners, _, strip_rows, order = tile_ref.shape
    tile = tile_ref[:, 0].astype(f32).reshape(owners * strip_rows, order)
    half = jnp.dot(left_ref[0], tile.astype(bf16), preferred_element_type=f32)
    shaped = jnp.dot(half.astype(bf16), right_ref[0], preferred_element_type=f32)
    ratio = jnp.sqrt(jnp.sum(tile * tile) / (jnp.sum(shaped * shaped) + epsilon))
    out_ref[:, 0] = (shaped * ratio).reshape(owners, strip_rows, order).astype(bf16)


def gram_tiles(tile_ref, left_ref, right_ref, new_left_ref, new_right_ref):
    owners, _, strip_rows, order = tile_ref.shape
    tile = tile_ref[:, 0].astype(f32).reshape(owners * strip_rows, order)
    low = tile.astype(bf16)
    turned = tile.T.astype(bf16)
    across = (((1,), (1,)), ((), ()))
    gram_rows = lax.dot_general(low, low, across, preferred_element_type=f32)
    new_left_ref[0] = beta_two * left_ref[0] + (1.0 - beta_two) * gram_rows
    gram_cols = lax.dot_general(turned, turned, across, preferred_element_type=f32)
    new_right_ref[0] = beta_two * right_ref[0] + (1.0 - beta_two) * gram_cols


def place(table_ref, in_ref, out_ref):
    owners, slots = in_ref.shape[:2]

    def body(owner, carry):
        for slot in range(slots):
            block = table_ref[owner * slots + slot]

            @pl.when(block >= 0)
            def _():
                out_ref[block] = in_ref[owner, slot]

        return carry

    lax.fori_loop(0, owners, body, 0, unroll=4)


def on_device(grads, left_stat, right_stat, left_root, right_root, slot_block):
    band = lax.axis_index("rep")
    bands = lax.axis_size("rep")
    owners = lax.axis_size("fsdp")
    block_rows, strip_rows, width = grads.shape[1:]
    slots, order = left_stat.shape[2:4]
    band_rows = block_rows // bands
    col_blocks = width // order
    blocks = band_rows * col_blocks
    half = band_rows // 2
    grads = grads.reshape(block_rows, strip_rows, width)

    up = [(i, (i + 1) % bands) for i in range(bands)]
    down = [(i, (i - 1) % bands) for i in range(bands)]

    def rows(step, part):
        start = lax.rem(band + step, bands) * band_rows + part * half
        return lax.dynamic_slice_in_dim(grads, start, half, axis=0)

    far_up = lax.ppermute(rows(2, 0), "rep", up)
    far_down = lax.ppermute(rows(2, 1), "rep", down)
    raw_up = lax.ppermute(rows(1, 1), "rep", up)
    raw_down = lax.ppermute(rows(bands - 1, 0), "rep", down)
    both_up = (rows(1, 0).astype(f32) + far_up.astype(f32)).astype(bf16)
    both_down = (rows(bands - 1, 1).astype(f32) + far_down.astype(f32)).astype(bf16)
    both_up = lax.ppermute(both_up, "rep", up)
    both_down = lax.ppermute(both_down, "rep", down)
    from_left = jnp.concatenate([both_up, raw_up], axis=0)
    from_right = jnp.concatenate([raw_down, both_down], axis=0)

    table = lax.dynamic_index_in_dim(slot_block, band, 0, keepdims=False).reshape(-1)
    outgoing = pl.pallas_call(
        sum_and_pick,
        out_shape=jax.ShapeDtypeStruct((owners, slots, strip_rows, order), bf16),
        grid_spec=pltpu.PrefetchScalarGridSpec(
            num_scalar_prefetch=2,
            grid=(1,),
            in_specs=[
                pl.BlockSpec((band_rows, strip_rows, width), lambda i, b, t: (b[0], 0, 0)),
                pl.BlockSpec((band_rows, strip_rows, width), lambda i, b, t: (0, 0, 0)),
                pl.BlockSpec((band_rows, strip_rows, width), lambda i, b, t: (0, 0, 0)),
            ],
            out_specs=pl.BlockSpec((owners, slots, strip_rows, order), lambda i, b, t: (0, 0, 0, 0)),
            scratch_shapes=[pltpu.VMEM((blocks + 1, strip_rows, order), bf16)],
        ),
        compiler_params=pltpu.CompilerParams(vmem_limit_bytes=vmem_bytes),
    )(band.reshape(1), table, grads, from_left, from_right)

    incoming = lax.all_to_all(outgoing, "fsdp", split_axis=0, concat_axis=0, tiled=True)

    strip_spec = pl.BlockSpec((owners, 1, strip_rows, order), lambda s: (0, s, 0, 0))
    square = pl.BlockSpec((1, order, order), lambda s: (s, 0, 0))
    scaled = pl.pallas_call(
        shape_tiles,
        out_shape=jax.ShapeDtypeStruct((owners, slots, strip_rows, order), bf16),
        grid=(slots,),
        in_specs=[strip_spec, square, square],
        out_specs=strip_spec,
        compiler_params=pltpu.CompilerParams(vmem_limit_bytes=vmem_bytes),
        cost_estimate=pl.CostEstimate(
            flops=4 * slots * order**3, bytes_accessed=8 * slots * order**2, transcendentals=0
        ),
    )(incoming, left_root[0, 0], right_root[0, 0])

    received = lax.all_to_all(scaled, "fsdp", split_axis=0, concat_axis=0, tiled=True)

    new_left, new_right = pl.pallas_call(
        gram_tiles,
        out_shape=[jax.ShapeDtypeStruct((slots, order, order), f32)] * 2,
        grid=(slots,),
        in_specs=[strip_spec, square, square],
        out_specs=[square, square],
        compiler_params=pltpu.CompilerParams(vmem_limit_bytes=vmem_bytes),
        cost_estimate=pl.CostEstimate(
            flops=4 * slots * order**3, bytes_accessed=18 * slots * order**2, transcendentals=0
        ),
    )(incoming, left_stat[0, 0], right_stat[0, 0])

    update = pl.pallas_call(
        place,
        out_shape=jax.ShapeDtypeStruct((blocks, strip_rows, order), bf16),
        grid_spec=pltpu.PrefetchScalarGridSpec(
            num_scalar_prefetch=1,
            grid=(1,),
            in_specs=[
                pl.BlockSpec((owners, slots, strip_rows, order), lambda i, t: (0, 0, 0, 0))
            ],
            out_specs=pl.BlockSpec((blocks, strip_rows, order), lambda i, t: (0, 0, 0)),
        ),
        compiler_params=pltpu.CompilerParams(vmem_limit_bytes=vmem_bytes),
    )(table, received)
    update = (
        update.reshape(band_rows, col_blocks, strip_rows, order)
        .transpose(0, 2, 1, 3)
        .reshape(band_rows, strip_rows, width)
    )
    return (new_left[None, None], new_right[None, None], update)


def solution(mesh):
    in_specs = (
        P("rep", None, "fsdp", None),
        P("rep", "fsdp", None, None, None),
        P("rep", "fsdp", None, None, None),
        P("rep", "fsdp", None, None, None),
        P("rep", "fsdp", None, None, None),
        P(),
    )
    out_specs = (
        P("rep", "fsdp", None, None, None),
        P("rep", "fsdp", None, None, None),
        P("rep", "fsdp", None),
    )
    return jax.shard_map(
        on_device, mesh=mesh, in_specs=in_specs, out_specs=out_specs, check_vma=False
    )
```

```python
import jax
import jax.numpy as jnp
from jax import lax
from jax.experimental import pallas as pl
from jax.experimental.pallas import tpu as pltpu
from jax.sharding import PartitionSpec as P

beta_two = 0.95
epsilon = 1e-06
f32 = jnp.float32
bf16 = jnp.bfloat16
vmem_bytes = 48 * 1024 * 1024


def add_far(band_ref, up_ref, down_ref, far_up_ref, far_down_ref, both_up_ref, both_down_ref):
    both_up_ref[...] = (up_ref[...].astype(f32) + far_up_ref[...].astype(f32)).astype(bf16)
    both_down_ref[...] = (down_ref[...].astype(f32) + far_down_ref[...].astype(f32)).astype(bf16)


def sum_and_pick(
    band_ref, table_ref, own_ref, both_up_ref, raw_down_ref, raw_up_ref, both_down_ref, out_ref, strips
):
    band_rows, strip_rows, width = own_ref.shape
    half = band_rows // 2
    order = strips.shape[2]
    col_blocks = width // order
    blocks = band_rows * col_blocks
    for row in range(band_rows):
        first, second = (both_up_ref, raw_down_ref) if row < half else (raw_up_ref, both_down_ref)
        total = (
            own_ref[row].astype(f32)
            + first[row % half].astype(f32)
            + second[row % half].astype(f32)
        ).astype(bf16)
        for col in range(col_blocks):
            strips[row * col_blocks + col] = total[:, col * order : (col + 1) * order]
    strips[blocks] = jnp.zeros((strip_rows, order), bf16)
    owners, slots = out_ref.shape[:2]

    def body(owner, carry):
        for slot in range(slots):
            block = table_ref[owner * slots + slot]
            out_ref[owner, slot] = strips[jnp.where(block >= 0, block, blocks)]
        return carry

    lax.fori_loop(0, owners, body, 0, unroll=4)


def shape_tiles(tile_ref, left_ref, right_ref, out_ref):
    owners, slots, strip_rows, order = tile_ref.shape
    for slot in range(slots):
        tile = tile_ref[:, slot].astype(f32).reshape(owners * strip_rows, order)
        half = jnp.dot(left_ref[slot], tile.astype(bf16), preferred_element_type=f32)
        shaped = jnp.dot(half.astype(bf16), right_ref[slot], preferred_element_type=f32)
        ratio = jnp.sqrt(jnp.sum(tile * tile) / (jnp.sum(shaped * shaped) + epsilon))
        out_ref[:, slot] = (shaped * ratio).reshape(owners, strip_rows, order).astype(bf16)


def gram_tiles(tile_ref, left_ref, right_ref, new_left_ref, new_right_ref):
    owners, _, strip_rows, order = tile_ref.shape
    tile = tile_ref[:, 0].astype(f32).reshape(owners * strip_rows, order)
    low = tile.astype(bf16)
    turned = tile.T.astype(bf16)
    across = (((1,), (1,)), ((), ()))
    gram_rows = lax.dot_general(low, low, across, preferred_element_type=f32)
    new_left_ref[0] = beta_two * left_ref[0] + (1.0 - beta_two) * gram_rows
    gram_cols = lax.dot_general(turned, turned, across, preferred_element_type=f32)
    new_right_ref[0] = beta_two * right_ref[0] + (1.0 - beta_two) * gram_cols


def place(locate_ref, in_ref, out_ref):
    slots = in_ref.shape[1]
    first = pl.program_id(0) * out_ref.shape[0]
    for block in range(out_ref.shape[0]):
        position = locate_ref[first + block]
        out_ref[block] = in_ref[position // slots, lax.rem(position, slots)]


def on_device(grads, left_stat, right_stat, left_root, right_root, slot_block):
    band = lax.axis_index("rep")
    bands = lax.axis_size("rep")
    owners = lax.axis_size("fsdp")
    block_rows, strip_rows, width = grads.shape[1:]
    slots, order = left_stat.shape[2:4]
    band_rows = block_rows // bands
    col_blocks = width // order
    blocks = band_rows * col_blocks
    half = band_rows // 2
    grads = grads.reshape(block_rows, strip_rows, width)

    up = [(i, (i + 1) % bands) for i in range(bands)]
    down = [(i, (i - 1) % bands) for i in range(bands)]

    band_number = band.reshape(1)
    half_shape = jax.ShapeDtypeStruct((half, strip_rows, width), bf16)
    whole = pl.BlockSpec(memory_space=pltpu.VMEM)

    def rows(source, step, part):
        start = lax.rem(band + step, bands) * band_rows + part * half
        return lax.dynamic_slice_in_dim(source, start, half, axis=0)

    far_up, far_down, later = lax.optimization_barrier(
        (rows(grads, 2, 0), rows(grads, 2, 1), grads)
    )
    raw_up, raw_down = rows(later, 1, 1), rows(later, bands - 1, 0)
    far_up = lax.ppermute(far_up, "rep", up)
    far_down = lax.ppermute(far_down, "rep", down)
    raw_up = lax.ppermute(raw_up, "rep", up)
    raw_down = lax.ppermute(raw_down, "rep", down)
    half_spec = pl.BlockSpec((half, strip_rows, width), lambda i, *s: (0, 0, 0))
    both_up, both_down = pl.pallas_call(
        add_far,
        out_shape=[half_shape] * 2,
        grid_spec=pltpu.PrefetchScalarGridSpec(
            num_scalar_prefetch=1,
            grid=(1,),
            in_specs=[
                pl.BlockSpec(
                    (half, strip_rows, width), lambda i, b: (lax.rem(b[0] + 1, bands) * 2, 0, 0)
                ),
                pl.BlockSpec(
                    (half, strip_rows, width),
                    lambda i, b: (lax.rem(b[0] + bands - 1, bands) * 2 + 1, 0, 0),
                ),
                half_spec,
                half_spec,
            ],
            out_specs=[half_spec] * 2,
        ),
        compiler_params=pltpu.CompilerParams(vmem_limit_bytes=vmem_bytes),
        cost_estimate=pl.CostEstimate(
            flops=0, bytes_accessed=64 * 1024 * 1024, transcendentals=0
        ),
    )(band_number, grads, grads, far_up, far_down)
    both_up = lax.ppermute(both_up, "rep", up)
    both_down = lax.ppermute(both_down, "rep", down)

    table = lax.dynamic_index_in_dim(slot_block, band, 0, keepdims=False).reshape(-1)
    positions = jnp.arange(owners * slots, dtype=jnp.int32)
    numbers = jnp.arange(blocks, dtype=jnp.int32)
    locate = jnp.sum(
        jnp.where(table[None, :] == numbers[:, None], positions[None, :], 0),
        axis=1,
        dtype=jnp.int32,
    )
    outgoing = pl.pallas_call(
        sum_and_pick,
        out_shape=jax.ShapeDtypeStruct((owners, slots, strip_rows, order), bf16),
        grid_spec=pltpu.PrefetchScalarGridSpec(
            num_scalar_prefetch=2,
            grid=(1,),
            in_specs=[
                pl.BlockSpec((band_rows, strip_rows, width), lambda i, b, t: (b[0], 0, 0)),
                half_spec,
                half_spec,
                half_spec,
                half_spec,
            ],
            out_specs=pl.BlockSpec((owners, slots, strip_rows, order), lambda i, b, t: (0, 0, 0, 0)),
            scratch_shapes=[pltpu.VMEM((blocks + 1, strip_rows, order), bf16)],
        ),
        compiler_params=pltpu.CompilerParams(vmem_limit_bytes=vmem_bytes),
    )(band_number, table, grads, both_up, raw_down, raw_up, both_down)

    incoming = lax.all_to_all(outgoing, "fsdp", split_axis=0, concat_axis=0, tiled=True)

    strip_spec = pl.BlockSpec((owners, 1, strip_rows, order), lambda s: (0, s, 0, 0))
    square = pl.BlockSpec((1, order, order), lambda s: (s, 0, 0))
    scaled = pl.pallas_call(
        shape_tiles,
        out_shape=jax.ShapeDtypeStruct((owners, slots, strip_rows, order), bf16),
        in_specs=[whole] * 3,
        out_specs=whole,
        compiler_params=pltpu.CompilerParams(vmem_limit_bytes=vmem_bytes),
        cost_estimate=pl.CostEstimate(
            flops=4 * slots * order**3, bytes_accessed=8 * slots * order**2, transcendentals=0
        ),
    )(incoming, left_root[0, 0], right_root[0, 0])

    received = lax.all_to_all(scaled, "fsdp", split_axis=0, concat_axis=0, tiled=True)

    new_left, new_right = pl.pallas_call(
        gram_tiles,
        out_shape=[jax.ShapeDtypeStruct((slots, order, order), f32)] * 2,
        grid=(slots,),
        in_specs=[strip_spec, square, square],
        out_specs=[square, square],
        compiler_params=pltpu.CompilerParams(vmem_limit_bytes=vmem_bytes),
        cost_estimate=pl.CostEstimate(
            flops=4 * slots * order**3, bytes_accessed=18 * slots * order**2, transcendentals=0
        ),
    )(incoming, left_stat[0, 0], right_stat[0, 0])

    update = pl.pallas_call(
        place,
        out_shape=jax.ShapeDtypeStruct((blocks, strip_rows, order), bf16),
        grid=(2,),
        in_specs=[pl.BlockSpec(memory_space=pltpu.SMEM), whole],
        out_specs=pl.BlockSpec((blocks // 2, strip_rows, order), lambda i: (i, 0, 0)),
        compiler_params=pltpu.CompilerParams(vmem_limit_bytes=vmem_bytes),
    )(locate, received)
    update = (
        update.reshape(band_rows, col_blocks, strip_rows, order)
        .transpose(0, 2, 1, 3)
        .reshape(band_rows, strip_rows, width)
    )
    return (new_left[None, None], new_right[None, None], update)


def solution(mesh):
    in_specs = (
        P("rep", None, "fsdp", None),
        P("rep", "fsdp", None, None, None),
        P("rep", "fsdp", None, None, None),
        P("rep", "fsdp", None, None, None),
        P("rep", "fsdp", None, None, None),
        P(),
    )
    out_specs = (
        P("rep", "fsdp", None, None, None),
        P("rep", "fsdp", None, None, None),
        P("rep", "fsdp", None),
    )
    return jax.shard_map(
        on_device, mesh=mesh, in_specs=in_specs, out_specs=out_specs, check_vma=False
    )
```

```python
import jax
import jax.numpy as jnp
from jax import lax
from jax.experimental import pallas as pl
from jax.experimental.pallas import tpu as pltpu
from jax.sharding import PartitionSpec as P

beta_two = 0.95
epsilon = 1e-06
f32 = jnp.float32
bf16 = jnp.bfloat16
vmem_bytes = 48 * 1024 * 1024
vmem_most = 60 * 1024 * 1024


def add_far(up_ref, down_ref, far_up_ref, far_down_ref, both_up_ref, both_down_ref):
    both_up_ref[...] = (up_ref[...].astype(f32) + far_up_ref[...].astype(f32)).astype(bf16)
    both_down_ref[...] = (down_ref[...].astype(f32) + far_down_ref[...].astype(f32)).astype(bf16)


def sum_and_pick(
    table_ref, own_ref, both_up_ref, raw_down_ref, raw_up_ref, both_down_ref, out_ref, strips
):
    band_rows, strip_rows, width = own_ref.shape
    half = band_rows // 2
    order = strips.shape[2]
    col_blocks = width // order
    blocks = band_rows * col_blocks
    for row in range(band_rows):
        first, second = (both_up_ref, raw_down_ref) if row < half else (raw_up_ref, both_down_ref)
        total = (
            own_ref[row].astype(f32)
            + first[row % half].astype(f32)
            + second[row % half].astype(f32)
        ).astype(bf16)
        for col in range(col_blocks):
            strips[row * col_blocks + col] = total[:, col * order : (col + 1) * order]
    strips[blocks] = jnp.zeros((strip_rows, order), bf16)
    owners, slots = out_ref.shape[:2]

    def body(owner, carry):
        for slot in range(slots):
            block = table_ref[owner * slots + slot]
            out_ref[owner, slot] = strips[jnp.where(block >= 0, block, blocks)]
        return carry

    lax.fori_loop(0, owners, body, 0, unroll=16)


def shape_tiles(tile_ref, left_ref, right_ref, out_ref):
    owners, slots, strip_rows, order = tile_ref.shape
    for slot in range(slots):
        low = tile_ref[:, slot].reshape(owners * strip_rows, order)
        half = jnp.dot(left_ref[slot], low, preferred_element_type=f32)
        shaped = jnp.dot(half.astype(bf16), right_ref[slot], preferred_element_type=f32)
        tile = low.astype(f32)
        ratio = jnp.sqrt(jnp.sum(tile * tile) / (jnp.sum(shaped * shaped) + epsilon))
        out_ref[:, slot] = (shaped * ratio).astype(bf16).reshape(owners, strip_rows, order)


def gram_tiles(tile_ref, left_ref, right_ref, new_left_ref, new_right_ref):
    owners, _, strip_rows, order = tile_ref.shape
    tile = tile_ref[:, 0].astype(f32).reshape(owners * strip_rows, order)
    low = tile.astype(bf16)
    turned = tile.T.astype(bf16)
    across = (((1,), (1,)), ((), ()))
    gram_rows = lax.dot_general(low, low, across, preferred_element_type=f32)
    new_left_ref[0] = beta_two * left_ref[0] + (1.0 - beta_two) * gram_rows
    gram_cols = lax.dot_general(turned, turned, across, preferred_element_type=f32)
    new_right_ref[0] = beta_two * right_ref[0] + (1.0 - beta_two) * gram_cols


def place(locate_ref, in_ref, out_ref):
    first = pl.program_id(0) * out_ref.shape[0]
    for block in range(out_ref.shape[0]):
        out_ref[block] = in_ref[locate_ref[first + block]]


def on_device(grads, left_stat, right_stat, left_root, right_root, slot_block):
    band = lax.axis_index("rep")
    bands = lax.axis_size("rep")
    owners = lax.axis_size("fsdp")
    block_rows, strip_rows, width = grads.shape[1:]
    slots, order = left_stat.shape[2:4]
    band_rows = block_rows // bands
    col_blocks = width // order
    blocks = band_rows * col_blocks
    half = band_rows // 2
    grads = grads.reshape(block_rows, strip_rows, width)

    up = [(i, (i + 1) % bands) for i in range(bands)]
    down = [(i, (i - 1) % bands) for i in range(bands)]

    half_shape = jax.ShapeDtypeStruct((half, strip_rows, width), bf16)
    whole = pl.BlockSpec(memory_space=pltpu.VMEM)

    def rows(source, step, part):
        start = lax.rem(band + step, bands) * band_rows + part * half
        return lax.dynamic_slice_in_dim(source, start, half, axis=0)

    far_up, far_down, later = lax.optimization_barrier(
        (rows(grads, 2, 0), rows(grads, 2, 1), grads)
    )
    raw_up, raw_down, later = lax.optimization_barrier(
        (rows(later, 1, 1), rows(later, bands - 1, 0), later)
    )
    next_up, next_down, later = lax.optimization_barrier(
        (rows(later, 1, 0), rows(later, bands - 1, 1), later)
    )
    own = lax.dynamic_slice_in_dim(later, band * band_rows, band_rows, axis=0)
    far_up = lax.ppermute(far_up, "rep", up)
    far_down = lax.ppermute(far_down, "rep", down)
    raw_up = lax.ppermute(raw_up, "rep", up)
    raw_down = lax.ppermute(raw_down, "rep", down)
    both_up, both_down = pl.pallas_call(
        add_far,
        out_shape=[half_shape] * 2,
        in_specs=[whole] * 4,
        out_specs=[whole] * 2,
        compiler_params=pltpu.CompilerParams(vmem_limit_bytes=vmem_bytes),
        cost_estimate=pl.CostEstimate(
            flops=0, bytes_accessed=64 * 1024 * 1024, transcendentals=0
        ),
    )(next_up, next_down, far_up, far_down)
    both_up = lax.ppermute(both_up, "rep", up)
    both_down = lax.ppermute(both_down, "rep", down)

    table = lax.dynamic_index_in_dim(slot_block, band, 0, keepdims=False).reshape(-1)
    positions = jnp.arange(owners * slots, dtype=jnp.int32)
    numbers = jnp.arange(blocks, dtype=jnp.int32)
    locate = jnp.sum(
        jnp.where(table[None, :] == numbers[:, None], positions[None, :], 0),
        axis=1,
        dtype=jnp.int32,
    )
    outgoing = pl.pallas_call(
        sum_and_pick,
        out_shape=jax.ShapeDtypeStruct((owners, slots, strip_rows, order), bf16),
        in_specs=[pl.BlockSpec(memory_space=pltpu.SMEM)] + [whole] * 5,
        out_specs=whole,
        scratch_shapes=[pltpu.VMEM((blocks + 1, strip_rows, order), bf16)],
        compiler_params=pltpu.CompilerParams(vmem_limit_bytes=vmem_bytes),
    )(table, own, both_up, raw_down, raw_up, both_down)

    incoming = lax.all_to_all(outgoing, "fsdp", split_axis=0, concat_axis=0, tiled=True)

    strip_spec = pl.BlockSpec((owners, 1, strip_rows, order), lambda s: (0, s, 0, 0))
    square = pl.BlockSpec((1, order, order), lambda s: (s, 0, 0))
    scaled = pl.pallas_call(
        shape_tiles,
        out_shape=jax.ShapeDtypeStruct((owners, slots, strip_rows, order), bf16),
        in_specs=[whole] * 3,
        out_specs=whole,
        compiler_params=pltpu.CompilerParams(vmem_limit_bytes=vmem_bytes),
        cost_estimate=pl.CostEstimate(
            flops=4 * slots * order**3, bytes_accessed=8 * slots * order**2, transcendentals=0
        ),
    )(incoming, left_root[0, 0], right_root[0, 0])

    received = lax.all_to_all(scaled, "fsdp", split_axis=0, concat_axis=0, tiled=True)

    new_left, new_right = pl.pallas_call(
        gram_tiles,
        out_shape=[jax.ShapeDtypeStruct((slots, order, order), f32)] * 2,
        grid=(slots,),
        in_specs=[strip_spec, square, square],
        out_specs=[square, square],
        compiler_params=pltpu.CompilerParams(vmem_limit_bytes=vmem_most),
        cost_estimate=pl.CostEstimate(
            flops=4 * slots * order**3, bytes_accessed=18 * slots * order**2, transcendentals=0
        ),
    )(incoming, left_stat[0, 0], right_stat[0, 0])

    update = pl.pallas_call(
        place,
        out_shape=jax.ShapeDtypeStruct((blocks, strip_rows, order), bf16),
        grid=(2,),
        in_specs=[pl.BlockSpec(memory_space=pltpu.SMEM), whole],
        out_specs=pl.BlockSpec((blocks // 2, strip_rows, order), lambda i: (i, 0, 0)),
        compiler_params=pltpu.CompilerParams(vmem_limit_bytes=vmem_bytes),
    )(locate, received.reshape(owners * slots, strip_rows, order))
    update = (
        update.reshape(band_rows, col_blocks, strip_rows, order)
        .transpose(0, 2, 1, 3)
        .reshape(band_rows, strip_rows, width)
    )
    return (new_left[None, None], new_right[None, None], update)


def solution(mesh):
    in_specs = (
        P("rep", None, "fsdp", None),
        P("rep", "fsdp", None, None, None),
        P("rep", "fsdp", None, None, None),
        P("rep", "fsdp", None, None, None),
        P("rep", "fsdp", None, None, None),
        P(),
    )
    out_specs = (
        P("rep", "fsdp", None, None, None),
        P("rep", "fsdp", None, None, None),
        P("rep", "fsdp", None),
    )
    return jax.shard_map(
        on_device, mesh=mesh, in_specs=in_specs, out_specs=out_specs, check_vma=False
    )
```

```python
import jax
import jax.numpy as jnp
from jax import lax
from jax.experimental import pallas as pl
from jax.experimental.pallas import tpu as pltpu
from jax.sharding import PartitionSpec as P

beta_two = 0.95
epsilon = 1e-06
f32 = jnp.float32
bf16 = jnp.bfloat16
vmem_bytes = 48 * 1024 * 1024
vmem_most = 60 * 1024 * 1024


def add_far(up_ref, down_ref, far_up_ref, far_down_ref, both_up_ref, both_down_ref):
    both_up_ref[...] = (up_ref[...].astype(f32) + far_up_ref[...].astype(f32)).astype(bf16)
    both_down_ref[...] = (down_ref[...].astype(f32) + far_down_ref[...].astype(f32)).astype(bf16)


def sum_and_send(
    locate_ref, own_ref, both_up_ref, raw_down_ref, raw_up_ref, both_down_ref, out_ref
):
    band_rows, strip_rows, width = own_ref.shape
    half = band_rows // 2
    order = out_ref.shape[2]
    col_blocks = width // order
    for row in range(band_rows):
        first, second = (both_up_ref, raw_down_ref) if row < half else (raw_up_ref, both_down_ref)
        for col in range(col_blocks):
            columns = slice(col * order, (col + 1) * order)
            total = (
                own_ref[row, :, columns].astype(f32)
                + first[row % half, :, columns].astype(f32)
                + second[row % half, :, columns].astype(f32)
            )
            out_ref[locate_ref[row * col_blocks + col]] = total.astype(bf16)


def shape_tiles(tile_ref, left_ref, right_ref, out_ref, scaled, sems):
    owners, slots, strip_rows, order = tile_ref.shape
    parts = scaled.shape[1]
    group = owners // parts
    copies = []
    for slot in range(slots):
        low = tile_ref[:, slot].reshape(owners * strip_rows, order)
        half = jnp.dot(left_ref[slot], low, preferred_element_type=f32)
        shaped = jnp.dot(half.astype(bf16), right_ref[slot], preferred_element_type=f32)
        tile = low.astype(f32)
        ratio = jnp.sqrt(jnp.sum(tile * tile) / (jnp.sum(shaped * shaped) + epsilon))
        for part in range(parts):
            rows = shaped[part * group * strip_rows : (part + 1) * group * strip_rows]
            scaled[slot, part] = (rows * ratio).astype(bf16).reshape(group, strip_rows, order)
            copy = pltpu.make_async_copy(
                scaled.at[slot, part],
                out_ref.at[pl.ds(part * group, group), slot],
                sems.at[slot * parts + part],
            )
            copy.start()
            copies.append(copy)
    for copy in copies:
        copy.wait()


def gram_tiles(held_ref, tile_ref, left_ref, right_ref, new_left_ref, new_right_ref):
    owners, _, strip_rows, order = tile_ref.shape
    tile = tile_ref[:, 0].astype(f32).reshape(owners * strip_rows, order)
    tile = jnp.where(held_ref[pl.program_id(0)] >= 0, tile, jnp.zeros_like(tile))
    low = tile.astype(bf16)
    turned = tile.T.astype(bf16)
    across = (((1,), (1,)), ((), ()))
    gram_rows = lax.dot_general(low, low, across, preferred_element_type=f32)
    new_left_ref[0] = beta_two * left_ref[0] + (1.0 - beta_two) * gram_rows
    gram_cols = lax.dot_general(turned, turned, across, preferred_element_type=f32)
    new_right_ref[0] = beta_two * right_ref[0] + (1.0 - beta_two) * gram_cols


def place(locate_ref, in_ref, out_ref):
    first = pl.program_id(0) * out_ref.shape[0]
    for block in range(out_ref.shape[0]):
        out_ref[block] = in_ref[locate_ref[first + block]]


def on_device(grads, left_stat, right_stat, left_root, right_root, slot_block):
    band = lax.axis_index("rep")
    bands = lax.axis_size("rep")
    owners = lax.axis_size("fsdp")
    block_rows, strip_rows, width = grads.shape[1:]
    slots, order = left_stat.shape[2:4]
    band_rows = block_rows // bands
    col_blocks = width // order
    blocks = band_rows * col_blocks
    half = band_rows // 2
    grads = grads.reshape(block_rows, strip_rows, width)

    up = [(i, (i + 1) % bands) for i in range(bands)]
    down = [(i, (i - 1) % bands) for i in range(bands)]

    half_shape = jax.ShapeDtypeStruct((half, strip_rows, width), bf16)
    whole = pl.BlockSpec(memory_space=pltpu.VMEM)

    def rows(source, step, part):
        start = lax.rem(band + step, bands) * band_rows + part * half
        return lax.dynamic_slice_in_dim(source, start, half, axis=0)

    far_up, far_down, later = lax.optimization_barrier(
        (rows(grads, 2, 0), rows(grads, 2, 1), grads)
    )
    raw_up, raw_down, later = lax.optimization_barrier(
        (rows(later, 1, 1), rows(later, bands - 1, 0), later)
    )
    next_up, next_down, later = lax.optimization_barrier(
        (rows(later, 1, 0), rows(later, bands - 1, 1), later)
    )
    own = lax.dynamic_slice_in_dim(later, band * band_rows, band_rows, axis=0)
    far_up = lax.ppermute(far_up, "rep", up)
    far_down = lax.ppermute(far_down, "rep", down)
    raw_up = lax.ppermute(raw_up, "rep", up)
    raw_down = lax.ppermute(raw_down, "rep", down)
    both_up, both_down = pl.pallas_call(
        add_far,
        out_shape=[half_shape] * 2,
        in_specs=[whole] * 4,
        out_specs=[whole] * 2,
        compiler_params=pltpu.CompilerParams(vmem_limit_bytes=vmem_bytes),
        cost_estimate=pl.CostEstimate(
            flops=0, bytes_accessed=64 * 1024 * 1024, transcendentals=0
        ),
    )(next_up, next_down, far_up, far_down)
    both_up = lax.ppermute(both_up, "rep", up)
    both_down = lax.ppermute(both_down, "rep", down)

    table = lax.dynamic_index_in_dim(slot_block, band, 0, keepdims=False).reshape(-1)
    held = lax.dynamic_slice_in_dim(table, lax.axis_index("fsdp") * slots, slots)
    positions = jnp.arange(owners * slots, dtype=jnp.int32)
    numbers = jnp.arange(blocks, dtype=jnp.int32)
    locate = jnp.sum(
        jnp.where(table[None, :] == numbers[:, None], positions[None, :], 0),
        axis=1,
        dtype=jnp.int32,
    )
    outgoing = pl.pallas_call(
        sum_and_send,
        out_shape=jax.ShapeDtypeStruct((owners * slots, strip_rows, order), bf16),
        in_specs=[pl.BlockSpec(memory_space=pltpu.SMEM)] + [whole] * 5,
        out_specs=whole,
        compiler_params=pltpu.CompilerParams(vmem_limit_bytes=vmem_bytes),
    )(locate, own, both_up, raw_down, raw_up, both_down)

    outgoing = outgoing.reshape(owners, slots, strip_rows, order)
    incoming = lax.all_to_all(outgoing, "fsdp", split_axis=0, concat_axis=0, tiled=True)

    strip_spec = pl.BlockSpec((owners, 1, strip_rows, order), lambda s: (0, s, 0, 0))
    square = pl.BlockSpec((1, order, order), lambda s: (s, 0, 0))
    scaled = pl.pallas_call(
        shape_tiles,
        out_shape=jax.ShapeDtypeStruct((owners, slots, strip_rows, order), bf16),
        in_specs=[whole] * 3,
        out_specs=pl.BlockSpec(memory_space=pl.ANY),
        scratch_shapes=[
            pltpu.VMEM((slots, 4, owners // 4, strip_rows, order), bf16),
            pltpu.SemaphoreType.DMA((slots * 4,)),
        ],
        compiler_params=pltpu.CompilerParams(vmem_limit_bytes=vmem_bytes),
        cost_estimate=pl.CostEstimate(
            flops=4 * slots * order**3, bytes_accessed=8 * slots * order**2, transcendentals=0
        ),
    )(incoming, left_root[0, 0], right_root[0, 0])

    received = lax.all_to_all(scaled, "fsdp", split_axis=0, concat_axis=0, tiled=True)

    new_left, new_right = pl.pallas_call(
        gram_tiles,
        out_shape=[jax.ShapeDtypeStruct((slots, order, order), f32)] * 2,
        grid=(slots,),
        in_specs=[pl.BlockSpec(memory_space=pltpu.SMEM), strip_spec, square, square],
        out_specs=[square, square],
        compiler_params=pltpu.CompilerParams(vmem_limit_bytes=vmem_most),
        cost_estimate=pl.CostEstimate(
            flops=4 * slots * order**3, bytes_accessed=18 * slots * order**2, transcendentals=0
        ),
    )(held, incoming, left_stat[0, 0], right_stat[0, 0])

    update = pl.pallas_call(
        place,
        out_shape=jax.ShapeDtypeStruct((blocks, strip_rows, order), bf16),
        grid=(2,),
        in_specs=[pl.BlockSpec(memory_space=pltpu.SMEM), whole],
        out_specs=pl.BlockSpec((blocks // 2, strip_rows, order), lambda i: (i, 0, 0)),
        compiler_params=pltpu.CompilerParams(vmem_limit_bytes=vmem_bytes),
    )(locate, received.reshape(owners * slots, strip_rows, order))
    update = (
        update.reshape(band_rows, col_blocks, strip_rows, order)
        .transpose(0, 2, 1, 3)
        .reshape(band_rows, strip_rows, width)
    )
    return (new_left[None, None], new_right[None, None], update)


def solution(mesh):
    in_specs = (
        P("rep", None, "fsdp", None),
        P("rep", "fsdp", None, None, None),
        P("rep", "fsdp", None, None, None),
        P("rep", "fsdp", None, None, None),
        P("rep", "fsdp", None, None, None),
        P(),
    )
    out_specs = (
        P("rep", "fsdp", None, None, None),
        P("rep", "fsdp", None, None, None),
        P("rep", "fsdp", None),
    )
    return jax.shard_map(
        on_device, mesh=mesh, in_specs=in_specs, out_specs=out_specs, check_vma=False
    )
```

```python
import jax
import jax.numpy as jnp
from jax import lax
from jax.experimental import pallas as pl
from jax.experimental.pallas import tpu as pltpu
from jax.sharding import PartitionSpec as P

beta_two = 0.95
epsilon = 1e-06
f32 = jnp.float32
bf16 = jnp.bfloat16
vmem_bytes = 48 * 1024 * 1024
vmem_most = 60 * 1024 * 1024


def add_far(up_ref, down_ref, far_up_ref, far_down_ref, both_up_ref, both_down_ref):
    both_up_ref[...] = (up_ref[...].astype(f32) + far_up_ref[...].astype(f32)).astype(bf16)
    both_down_ref[...] = (down_ref[...].astype(f32) + far_down_ref[...].astype(f32)).astype(bf16)


def sum_and_send(
    locate_ref, own_ref, both_up_ref, raw_down_ref, raw_up_ref, both_down_ref, out_ref
):
    band_rows, strip_rows, width = own_ref.shape
    half = band_rows // 2
    order = out_ref.shape[2]
    col_blocks = width // order
    places = locate_ref[...]
    for row in range(band_rows):
        first, second = (both_up_ref, raw_down_ref) if row < half else (raw_up_ref, both_down_ref)
        for col in range(col_blocks):
            columns = slice(col * order, (col + 1) * order)
            total = (
                own_ref[row, :, columns].astype(f32)
                + first[row % half, :, columns].astype(f32)
                + second[row % half, :, columns].astype(f32)
            )
            out_ref[places[0, row * col_blocks + col]] = total.astype(bf16)


def shape_tiles(tile_ref, left_ref, right_ref, out_ref, scaled, sems):
    owners, slots, strip_rows, order = tile_ref.shape
    parts = scaled.shape[1]
    group = owners // parts
    copies = []
    for slot in range(slots):
        low = tile_ref[:, slot].reshape(owners * strip_rows, order)
        half = jnp.dot(left_ref[slot], low, preferred_element_type=f32)
        shaped = jnp.dot(half.astype(bf16), right_ref[slot], preferred_element_type=f32)
        tile = low.astype(f32)
        ratio = jnp.sqrt(jnp.sum(tile * tile) / (jnp.sum(shaped * shaped) + epsilon))
        for part in range(parts):
            rows = shaped[part * group * strip_rows : (part + 1) * group * strip_rows]
            scaled[slot, part] = (rows * ratio).astype(bf16).reshape(group, strip_rows, order)
            copy = pltpu.make_async_copy(
                scaled.at[slot, part],
                out_ref.at[pl.ds(part * group, group), slot],
                sems.at[slot * parts + part],
            )
            copy.start()
            copies.append(copy)
    for copy in copies:
        copy.wait()


def gram_tiles(held_ref, tile_ref, left_ref, right_ref, new_left_ref, new_right_ref):
    owners, _, strip_rows, order = tile_ref.shape
    tile = tile_ref[:, 0].astype(f32).reshape(owners * strip_rows, order)
    tile = jnp.where(held_ref[pl.program_id(0)] >= 0, tile, jnp.zeros_like(tile))
    low = tile.astype(bf16)
    turned = tile.T.astype(bf16)
    across = (((1,), (1,)), ((), ()))
    gram_rows = lax.dot_general(low, low, across, preferred_element_type=f32)
    new_left_ref[0] = beta_two * left_ref[0] + (1.0 - beta_two) * gram_rows
    gram_cols = lax.dot_general(turned, turned, across, preferred_element_type=f32)
    new_right_ref[0] = beta_two * right_ref[0] + (1.0 - beta_two) * gram_cols


def place(locate_ref, in_ref, out_ref, placed, sems):
    parts, group = placed.shape[:2]
    places = locate_ref[...]
    copies = []
    for part in range(parts):
        for index in range(group):
            placed[part, index] = in_ref[places[0, part * group + index]]
        copy = pltpu.make_async_copy(
            placed.at[part], out_ref.at[pl.ds(part * group, group)], sems.at[part]
        )
        copy.start()
        copies.append(copy)
    for copy in copies:
        copy.wait()


def on_device(grads, left_stat, right_stat, left_root, right_root, slot_block):
    band = lax.axis_index("rep")
    bands = lax.axis_size("rep")
    owners = lax.axis_size("fsdp")
    block_rows, strip_rows, width = grads.shape[1:]
    slots, order = left_stat.shape[2:4]
    band_rows = block_rows // bands
    col_blocks = width // order
    blocks = band_rows * col_blocks
    half = band_rows // 2
    grads = grads.reshape(block_rows, strip_rows, width)

    up = [(i, (i + 1) % bands) for i in range(bands)]
    down = [(i, (i - 1) % bands) for i in range(bands)]

    half_shape = jax.ShapeDtypeStruct((half, strip_rows, width), bf16)
    whole = pl.BlockSpec(memory_space=pltpu.VMEM)

    def rows(source, step, part):
        start = lax.rem(band + step, bands) * band_rows + part * half
        return lax.dynamic_slice_in_dim(source, start, half, axis=0)

    far_up, far_down, later = lax.optimization_barrier(
        (rows(grads, 2, 0), rows(grads, 2, 1), grads)
    )
    raw_up, raw_down, later = lax.optimization_barrier(
        (rows(later, 1, 1), rows(later, bands - 1, 0), later)
    )
    next_up, next_down, later = lax.optimization_barrier(
        (rows(later, 1, 0), rows(later, bands - 1, 1), later)
    )
    own = lax.dynamic_slice_in_dim(later, band * band_rows, band_rows, axis=0)
    far_up = lax.ppermute(far_up, "rep", up)
    far_down = lax.ppermute(far_down, "rep", down)
    raw_up = lax.ppermute(raw_up, "rep", up)
    raw_down = lax.ppermute(raw_down, "rep", down)
    both_up, both_down = pl.pallas_call(
        add_far,
        out_shape=[half_shape] * 2,
        in_specs=[whole] * 4,
        out_specs=[whole] * 2,
        compiler_params=pltpu.CompilerParams(vmem_limit_bytes=vmem_bytes),
        cost_estimate=pl.CostEstimate(
            flops=0, bytes_accessed=64 * 1024 * 1024, transcendentals=0
        ),
    )(next_up, next_down, far_up, far_down)
    both_up = lax.ppermute(both_up, "rep", up)
    both_down = lax.ppermute(both_down, "rep", down)

    table = lax.dynamic_index_in_dim(slot_block, band, 0, keepdims=False).reshape(-1)
    held = lax.dynamic_slice_in_dim(table, lax.axis_index("fsdp") * slots, slots)
    positions = jnp.arange(owners * slots, dtype=jnp.int32)
    numbers = jnp.arange(blocks, dtype=jnp.int32)
    locate = jnp.sum(
        jnp.where(table[None, :] == numbers[:, None], positions[None, :], 0),
        axis=1,
        dtype=jnp.int32,
    ).reshape(1, blocks)
    outgoing = pl.pallas_call(
        sum_and_send,
        out_shape=jax.ShapeDtypeStruct((owners * slots, strip_rows, order), bf16),
        in_specs=[whole] * 6,
        out_specs=whole,
        compiler_params=pltpu.CompilerParams(vmem_limit_bytes=vmem_bytes),
    )(locate, own, both_up, raw_down, raw_up, both_down)

    outgoing = outgoing.reshape(owners, slots, strip_rows, order)
    incoming = lax.all_to_all(outgoing, "fsdp", split_axis=0, concat_axis=0, tiled=True)

    strip_spec = pl.BlockSpec((owners, 1, strip_rows, order), lambda s: (0, s, 0, 0))
    square = pl.BlockSpec((1, order, order), lambda s: (s, 0, 0))
    scaled = pl.pallas_call(
        shape_tiles,
        out_shape=jax.ShapeDtypeStruct((owners, slots, strip_rows, order), bf16),
        in_specs=[whole] * 3,
        out_specs=pl.BlockSpec(memory_space=pl.ANY),
        scratch_shapes=[
            pltpu.VMEM((slots, 4, owners // 4, strip_rows, order), bf16),
            pltpu.SemaphoreType.DMA((slots * 4,)),
        ],
        compiler_params=pltpu.CompilerParams(vmem_limit_bytes=vmem_bytes),
        cost_estimate=pl.CostEstimate(
            flops=4 * slots * order**3, bytes_accessed=8 * slots * order**2, transcendentals=0
        ),
    )(incoming, left_root[0, 0], right_root[0, 0])

    received = lax.all_to_all(scaled, "fsdp", split_axis=0, concat_axis=0, tiled=True)

    new_left, new_right = pl.pallas_call(
        gram_tiles,
        out_shape=[jax.ShapeDtypeStruct((slots, order, order), f32)] * 2,
        grid=(slots,),
        in_specs=[pl.BlockSpec(memory_space=pltpu.SMEM), strip_spec, square, square],
        out_specs=[square, square],
        compiler_params=pltpu.CompilerParams(vmem_limit_bytes=vmem_most),
        cost_estimate=pl.CostEstimate(
            flops=4 * slots * order**3, bytes_accessed=18 * slots * order**2, transcendentals=0
        ),
    )(held, incoming, left_stat[0, 0], right_stat[0, 0])

    update = pl.pallas_call(
        place,
        out_shape=jax.ShapeDtypeStruct((blocks, strip_rows, order), bf16),
        in_specs=[whole] * 2,
        out_specs=pl.BlockSpec(memory_space=pl.ANY),
        scratch_shapes=[
            pltpu.VMEM((2, blocks // 2, strip_rows, order), bf16),
            pltpu.SemaphoreType.DMA((2,)),
        ],
        compiler_params=pltpu.CompilerParams(vmem_limit_bytes=vmem_bytes),
    )(locate, received.reshape(owners * slots, strip_rows, order))
    update = (
        update.reshape(band_rows, col_blocks, strip_rows, order)
        .transpose(0, 2, 1, 3)
        .reshape(band_rows, strip_rows, width)
    )
    return (new_left[None, None], new_right[None, None], update)


def solution(mesh):
    in_specs = (
        P("rep", None, "fsdp", None),
        P("rep", "fsdp", None, None, None),
        P("rep", "fsdp", None, None, None),
        P("rep", "fsdp", None, None, None),
        P("rep", "fsdp", None, None, None),
        P(),
    )
    out_specs = (
        P("rep", "fsdp", None, None, None),
        P("rep", "fsdp", None, None, None),
        P("rep", "fsdp", None),
    )
    return jax.shard_map(
        on_device, mesh=mesh, in_specs=in_specs, out_specs=out_specs, check_vma=False
    )
```

```python
import jax
import jax.numpy as jnp
from jax import lax
from jax.experimental import pallas as pl
from jax.experimental.pallas import tpu as pltpu
from jax.sharding import PartitionSpec as P

beta_two = 0.95
epsilon = 1e-06
f32 = jnp.float32
bf16 = jnp.bfloat16
vmem_bytes = 48 * 1024 * 1024
vmem_most = 60 * 1024 * 1024


def add_far(next_ref, far_ref, both_ref):
    both_ref[...] = (next_ref[...].astype(f32) + far_ref[...].astype(f32)).astype(bf16)


def sum_and_send(
    locate_ref, own_ref, both_up_ref, raw_down_ref, raw_up_ref, both_down_ref, out_ref
):
    band_rows, strip_rows, width = own_ref.shape
    half = band_rows // 2
    order = out_ref.shape[2]
    col_blocks = width // order
    places = locate_ref[...]
    for row in range(band_rows):
        first, second = (both_up_ref, raw_down_ref) if row < half else (raw_up_ref, both_down_ref)
        for col in range(col_blocks):
            columns = slice(col * order, (col + 1) * order)
            total = (
                own_ref[row, :, columns].astype(f32)
                + first[row % half, :, columns].astype(f32)
                + second[row % half, :, columns].astype(f32)
            )
            out_ref[places[0, row * col_blocks + col]] = total.astype(bf16)


def shape_tiles(tile_ref, left_ref, right_ref, out_ref, scaled, sems):
    owners, slots, strip_rows, order = tile_ref.shape
    parts = scaled.shape[1]
    group = owners // parts
    copies = []
    lows = [tile_ref[:, slot].reshape(owners * strip_rows, order) for slot in range(slots)]
    halves = [
        jnp.dot(left_ref[slot], lows[slot], preferred_element_type=f32).astype(bf16)
        for slot in range(slots)
    ]
    for slot in range(slots):
        shaped = jnp.dot(halves[slot], right_ref[slot], preferred_element_type=f32)
        tile = lows[slot].astype(f32)
        ratio = jnp.sqrt(jnp.sum(tile * tile) / (jnp.sum(shaped * shaped) + epsilon))
        for part in range(parts):
            rows = shaped[part * group * strip_rows : (part + 1) * group * strip_rows]
            scaled[slot, part] = (rows * ratio).astype(bf16).reshape(group, strip_rows, order)
            copy = pltpu.make_async_copy(
                scaled.at[slot, part],
                out_ref.at[pl.ds(part * group, group), slot],
                sems.at[slot * parts + part],
            )
            copy.start()
            copies.append(copy)
    for copy in copies:
        copy.wait()


def gram_tiles(held_ref, tile_ref, left_ref, right_ref, new_left_ref, new_right_ref):
    owners, _, strip_rows, order = tile_ref.shape
    tile = tile_ref[:, 0].astype(f32).reshape(owners * strip_rows, order)
    tile = jnp.where(held_ref[pl.program_id(0)] >= 0, tile, jnp.zeros_like(tile))
    low = tile.astype(bf16)
    turned = tile.T.astype(bf16)
    across = (((1,), (1,)), ((), ()))
    gram_rows = lax.dot_general(low, low, across, preferred_element_type=f32)
    new_left_ref[0] = beta_two * left_ref[0] + (1.0 - beta_two) * gram_rows
    gram_cols = lax.dot_general(turned, turned, across, preferred_element_type=f32)
    new_right_ref[0] = beta_two * right_ref[0] + (1.0 - beta_two) * gram_cols


def place(locate_ref, in_ref, out_ref, placed, sems):
    parts, group = placed.shape[:2]
    places = locate_ref[...]
    copies = []
    for part in range(parts):
        for index in range(group):
            placed[part, index] = in_ref[places[0, part * group + index]]
        copy = pltpu.make_async_copy(
            placed.at[part], out_ref.at[pl.ds(part * group, group)], sems.at[part]
        )
        copy.start()
        copies.append(copy)
    for copy in copies:
        copy.wait()


def on_device(grads, left_stat, right_stat, left_root, right_root, slot_block):
    band = lax.axis_index("rep")
    bands = lax.axis_size("rep")
    owners = lax.axis_size("fsdp")
    block_rows, strip_rows, width = grads.shape[1:]
    slots, order = left_stat.shape[2:4]
    band_rows = block_rows // bands
    col_blocks = width // order
    blocks = band_rows * col_blocks
    half = band_rows // 2
    grads = grads.reshape(block_rows, strip_rows, width)

    up = [(i, (i + 1) % bands) for i in range(bands)]
    down = [(i, (i - 1) % bands) for i in range(bands)]

    half_shape = jax.ShapeDtypeStruct((half, strip_rows, width), bf16)
    whole = pl.BlockSpec(memory_space=pltpu.VMEM)

    def rows(source, step, part):
        start = lax.rem(band + step, bands) * band_rows + part * half
        return lax.dynamic_slice_in_dim(source, start, half, axis=0)

    far_up, far_down, later = lax.optimization_barrier(
        (rows(grads, 2, 0), rows(grads, 2, 1), grads)
    )
    raw_up, raw_down, later = lax.optimization_barrier(
        (rows(later, 1, 1), rows(later, bands - 1, 0), later)
    )
    next_up, next_down, later = lax.optimization_barrier(
        (rows(later, 1, 0), rows(later, bands - 1, 1), later)
    )
    own = lax.dynamic_slice_in_dim(later, band * band_rows, band_rows, axis=0)
    far_up = lax.ppermute(far_up, "rep", up)
    far_down = lax.ppermute(far_down, "rep", down)
    raw_up = lax.ppermute(raw_up, "rep", up)
    raw_down = lax.ppermute(raw_down, "rep", down)
    both_up, both_down = (
        pl.pallas_call(
            add_far,
            out_shape=half_shape,
            in_specs=[whole] * 2,
            out_specs=whole,
            compiler_params=pltpu.CompilerParams(vmem_limit_bytes=vmem_bytes),
            cost_estimate=pl.CostEstimate(
                flops=0, bytes_accessed=32 * 1024 * 1024, transcendentals=0
            ),
        )(after, far)
        for after, far in ((next_up, far_up), (next_down, far_down))
    )
    both_up = lax.ppermute(both_up, "rep", up)
    both_down = lax.ppermute(both_down, "rep", down)

    table = lax.dynamic_index_in_dim(slot_block, band, 0, keepdims=False).reshape(-1)
    held = lax.dynamic_slice_in_dim(table, lax.axis_index("fsdp") * slots, slots)
    positions = jnp.arange(owners * slots, dtype=jnp.int32)
    numbers = jnp.arange(blocks, dtype=jnp.int32)
    locate = jnp.sum(
        jnp.where(table[None, :] == numbers[:, None], positions[None, :], 0),
        axis=1,
        dtype=jnp.int32,
    ).reshape(1, blocks)
    outgoing = pl.pallas_call(
        sum_and_send,
        out_shape=jax.ShapeDtypeStruct((owners * slots, strip_rows, order), bf16),
        in_specs=[whole] * 6,
        out_specs=whole,
        compiler_params=pltpu.CompilerParams(vmem_limit_bytes=vmem_bytes),
    )(locate, own, both_up, raw_down, raw_up, both_down)

    outgoing = outgoing.reshape(owners, slots, strip_rows, order)
    incoming = lax.all_to_all(outgoing, "fsdp", split_axis=0, concat_axis=0, tiled=True)

    strip_spec = pl.BlockSpec((owners, 1, strip_rows, order), lambda s: (0, s, 0, 0))
    square = pl.BlockSpec((1, order, order), lambda s: (s, 0, 0))
    scaled = pl.pallas_call(
        shape_tiles,
        out_shape=jax.ShapeDtypeStruct((owners, slots, strip_rows, order), bf16),
        in_specs=[whole] * 3,
        out_specs=pl.BlockSpec(memory_space=pl.ANY),
        scratch_shapes=[
            pltpu.VMEM((slots, 2, owners // 2, strip_rows, order), bf16),
            pltpu.SemaphoreType.DMA((slots * 2,)),
        ],
        compiler_params=pltpu.CompilerParams(vmem_limit_bytes=vmem_bytes),
        cost_estimate=pl.CostEstimate(
            flops=4 * slots * order**3, bytes_accessed=8 * slots * order**2, transcendentals=0
        ),
    )(incoming, left_root[0, 0], right_root[0, 0])

    received = lax.all_to_all(scaled, "fsdp", split_axis=0, concat_axis=0, tiled=True)

    new_left, new_right = pl.pallas_call(
        gram_tiles,
        out_shape=[jax.ShapeDtypeStruct((slots, order, order), f32)] * 2,
        grid=(slots,),
        in_specs=[pl.BlockSpec(memory_space=pltpu.SMEM), strip_spec, square, square],
        out_specs=[square, square],
        compiler_params=pltpu.CompilerParams(vmem_limit_bytes=vmem_most),
        cost_estimate=pl.CostEstimate(
            flops=4 * slots * order**3, bytes_accessed=18 * slots * order**2, transcendentals=0
        ),
    )(held, incoming, left_stat[0, 0], right_stat[0, 0])

    update = pl.pallas_call(
        place,
        out_shape=jax.ShapeDtypeStruct((blocks, strip_rows, order), bf16),
        in_specs=[whole] * 2,
        out_specs=pl.BlockSpec(memory_space=pl.ANY),
        scratch_shapes=[
            pltpu.VMEM((2, blocks // 2, strip_rows, order), bf16),
            pltpu.SemaphoreType.DMA((2,)),
        ],
        compiler_params=pltpu.CompilerParams(vmem_limit_bytes=vmem_bytes),
    )(locate, received.reshape(owners * slots, strip_rows, order))
    update = (
        update.reshape(band_rows, col_blocks, strip_rows, order)
        .transpose(0, 2, 1, 3)
        .reshape(band_rows, strip_rows, width)
    )
    return (new_left[None, None], new_right[None, None], update)


def solution(mesh):
    in_specs = (
        P("rep", None, "fsdp", None),
        P("rep", "fsdp", None, None, None),
        P("rep", "fsdp", None, None, None),
        P("rep", "fsdp", None, None, None),
        P("rep", "fsdp", None, None, None),
        P(),
    )
    out_specs = (
        P("rep", "fsdp", None, None, None),
        P("rep", "fsdp", None, None, None),
        P("rep", "fsdp", None),
    )
    return jax.shard_map(
        on_device, mesh=mesh, in_specs=in_specs, out_specs=out_specs, check_vma=False
    )
```

```python
import jax
import jax.numpy as jnp
from jax import lax
from jax.experimental import pallas as pl
from jax.experimental.pallas import tpu as pltpu
from jax.sharding import PartitionSpec as P

beta_two = 0.95
epsilon = 1e-06
f32 = jnp.float32
bf16 = jnp.bfloat16
vmem_bytes = 20 * 1024 * 1024
vmem_most = 60 * 1024 * 1024


def add_far(up_ref, down_ref, far_up_ref, far_down_ref, both_up_ref, both_down_ref):
    both_up_ref[...] = (up_ref[...].astype(f32) + far_up_ref[...].astype(f32)).astype(bf16)
    both_down_ref[...] = (down_ref[...].astype(f32) + far_down_ref[...].astype(f32)).astype(bf16)


def sum_and_send(
    locate_ref, own_ref, both_up_ref, raw_down_ref, raw_up_ref, both_down_ref, out_ref
):
    band_rows, strip_rows, width = own_ref.shape
    half = band_rows // 2
    order = out_ref.shape[2]
    col_blocks = width // order
    places = locate_ref[...]
    for row in range(band_rows):
        first, second = (both_up_ref, raw_down_ref) if row < half else (raw_up_ref, both_down_ref)
        for col in range(col_blocks):
            columns = slice(col * order, (col + 1) * order)
            total = (
                own_ref[row, :, columns].astype(f32)
                + first[row % half, :, columns].astype(f32)
                + second[row % half, :, columns].astype(f32)
            )
            out_ref[places[0, row * col_blocks + col]] = total.astype(bf16)


def shape_tiles(tile_ref, left_ref, right_ref, out_ref, scaled, sems):
    owners, slots, strip_rows, order = tile_ref.shape
    parts = scaled.shape[1]
    group = owners // parts
    copies = []
    for slot in range(slots):
        low = tile_ref[:, slot].reshape(owners * strip_rows, order)
        half = jnp.dot(left_ref[slot], low, preferred_element_type=f32)
        shaped = jnp.dot(half.astype(bf16), right_ref[slot], preferred_element_type=f32)
        tile = low.astype(f32)
        ratio = jnp.sqrt(jnp.sum(tile * tile) / (jnp.sum(shaped * shaped) + epsilon))
        for part in range(parts):
            rows = shaped[part * group * strip_rows : (part + 1) * group * strip_rows]
            scaled[slot, part] = (rows * ratio).astype(bf16).reshape(group, strip_rows, order)
            copy = pltpu.make_async_copy(
                scaled.at[slot, part],
                out_ref.at[pl.ds(part * group, group), slot],
                sems.at[slot * parts + part],
            )
            copy.start()
            copies.append(copy)
    for copy in copies:
        copy.wait()


def gram_tiles(held_ref, tile_ref, left_ref, right_ref, new_left_ref, new_right_ref):
    owners, _, strip_rows, order = tile_ref.shape
    tile = tile_ref[:, 0].astype(f32).reshape(owners * strip_rows, order)
    tile = jnp.where(held_ref[pl.program_id(0)] >= 0, tile, jnp.zeros_like(tile))
    low = tile.astype(bf16)
    turned = tile.T.astype(bf16)
    across = (((1,), (1,)), ((), ()))
    gram_rows = lax.dot_general(low, low, across, preferred_element_type=f32)
    new_left_ref[0] = beta_two * left_ref[0] + (1.0 - beta_two) * gram_rows
    gram_cols = lax.dot_general(turned, turned, across, preferred_element_type=f32)
    new_right_ref[0] = beta_two * right_ref[0] + (1.0 - beta_two) * gram_cols


def place(locate_ref, in_ref, out_ref, placed, sems):
    parts, group = placed.shape[:2]
    places = locate_ref[...]
    copies = []
    for part in range(parts):
        for index in range(group):
            placed[part, index] = in_ref[places[0, part * group + index]]
        copy = pltpu.make_async_copy(
            placed.at[part], out_ref.at[pl.ds(part * group, group)], sems.at[part]
        )
        copy.start()
        copies.append(copy)
    for copy in copies:
        copy.wait()


def on_device(grads, left_stat, right_stat, left_root, right_root, slot_block):
    band = lax.axis_index("rep")
    bands = lax.axis_size("rep")
    owners = lax.axis_size("fsdp")
    block_rows, strip_rows, width = grads.shape[1:]
    slots, order = left_stat.shape[2:4]
    band_rows = block_rows // bands
    col_blocks = width // order
    blocks = band_rows * col_blocks
    half = band_rows // 2
    grads = grads.reshape(block_rows, strip_rows, width)

    up = [(i, (i + 1) % bands) for i in range(bands)]
    down = [(i, (i - 1) % bands) for i in range(bands)]

    half_shape = jax.ShapeDtypeStruct((half, strip_rows, width), bf16)
    whole = pl.BlockSpec(memory_space=pltpu.VMEM)

    def rows(source, step, part):
        start = lax.rem(band + step, bands) * band_rows + part * half
        return lax.dynamic_slice_in_dim(source, start, half, axis=0)

    far_up, far_down, later = lax.optimization_barrier(
        (rows(grads, 2, 0), rows(grads, 2, 1), grads)
    )
    raw_up, raw_down, later = lax.optimization_barrier(
        (rows(later, 1, 1), rows(later, bands - 1, 0), later)
    )
    next_up, next_down, later = lax.optimization_barrier(
        (rows(later, 1, 0), rows(later, bands - 1, 1), later)
    )
    own = lax.dynamic_slice_in_dim(later, band * band_rows, band_rows, axis=0)
    far_up = lax.ppermute(far_up, "rep", up)
    far_down = lax.ppermute(far_down, "rep", down)
    raw_up = lax.ppermute(raw_up, "rep", up)
    raw_down = lax.ppermute(raw_down, "rep", down)
    both_up, both_down = pl.pallas_call(
        add_far,
        out_shape=[half_shape] * 2,
        in_specs=[whole] * 4,
        out_specs=[whole] * 2,
        compiler_params=pltpu.CompilerParams(vmem_limit_bytes=vmem_bytes),
        cost_estimate=pl.CostEstimate(
            flops=0, bytes_accessed=64 * 1024 * 1024, transcendentals=0
        ),
    )(next_up, next_down, far_up, far_down)
    both_up = lax.ppermute(both_up, "rep", up)
    both_down = lax.ppermute(both_down, "rep", down)

    table = lax.dynamic_index_in_dim(slot_block, band, 0, keepdims=False).reshape(-1)
    held = lax.dynamic_slice_in_dim(table, lax.axis_index("fsdp") * slots, slots)
    positions = jnp.arange(owners * slots, dtype=jnp.int32)
    numbers = jnp.arange(blocks, dtype=jnp.int32)
    locate = jnp.sum(
        jnp.where(table[None, :] == numbers[:, None], positions[None, :], 0),
        axis=1,
        dtype=jnp.int32,
    ).reshape(1, blocks)
    outgoing = pl.pallas_call(
        sum_and_send,
        out_shape=jax.ShapeDtypeStruct((owners * slots, strip_rows, order), bf16),
        in_specs=[whole] * 6,
        out_specs=whole,
        compiler_params=pltpu.CompilerParams(vmem_limit_bytes=vmem_bytes),
    )(locate, own, both_up, raw_down, raw_up, both_down)

    outgoing = outgoing.reshape(owners, slots, strip_rows, order)
    incoming = lax.all_to_all(outgoing, "fsdp", split_axis=0, concat_axis=0, tiled=True)

    strip_spec = pl.BlockSpec((owners, 1, strip_rows, order), lambda s: (0, s, 0, 0))
    square = pl.BlockSpec((1, order, order), lambda s: (s, 0, 0))
    scaled = pl.pallas_call(
        shape_tiles,
        out_shape=jax.ShapeDtypeStruct((owners, slots, strip_rows, order), bf16),
        in_specs=[whole] * 3,
        out_specs=pl.BlockSpec(memory_space=pl.ANY),
        scratch_shapes=[
            pltpu.VMEM((slots, 4, owners // 4, strip_rows, order), bf16),
            pltpu.SemaphoreType.DMA((slots * 4,)),
        ],
        compiler_params=pltpu.CompilerParams(vmem_limit_bytes=vmem_bytes),
        cost_estimate=pl.CostEstimate(
            flops=4 * slots * order**3, bytes_accessed=8 * slots * order**2, transcendentals=0
        ),
    )(incoming, left_root[0, 0], right_root[0, 0])

    received = lax.all_to_all(scaled, "fsdp", split_axis=0, concat_axis=0, tiled=True)

    new_left, new_right = pl.pallas_call(
        gram_tiles,
        out_shape=[jax.ShapeDtypeStruct((slots, order, order), f32)] * 2,
        grid=(slots,),
        in_specs=[pl.BlockSpec(memory_space=pltpu.SMEM), strip_spec, square, square],
        out_specs=[square, square],
        compiler_params=pltpu.CompilerParams(vmem_limit_bytes=vmem_most),
        cost_estimate=pl.CostEstimate(
            flops=4 * slots * order**3, bytes_accessed=18 * slots * order**2, transcendentals=0
        ),
    )(held, incoming, left_stat[0, 0], right_stat[0, 0])

    update = pl.pallas_call(
        place,
        out_shape=jax.ShapeDtypeStruct((blocks, strip_rows, order), bf16),
        in_specs=[whole] * 2,
        out_specs=pl.BlockSpec(memory_space=pl.ANY),
        scratch_shapes=[
            pltpu.VMEM((2, blocks // 2, strip_rows, order), bf16),
            pltpu.SemaphoreType.DMA((2,)),
        ],
        compiler_params=pltpu.CompilerParams(vmem_limit_bytes=vmem_bytes),
    )(locate, received.reshape(owners * slots, strip_rows, order))
    update = (
        update.reshape(band_rows, col_blocks, strip_rows, order)
        .transpose(0, 2, 1, 3)
        .reshape(band_rows, strip_rows, width)
    )
    return (new_left[None, None], new_right[None, None], update)


def solution(mesh):
    in_specs = (
        P("rep", None, "fsdp", None),
        P("rep", "fsdp", None, None, None),
        P("rep", "fsdp", None, None, None),
        P("rep", "fsdp", None, None, None),
        P("rep", "fsdp", None, None, None),
        P(),
    )
    out_specs = (
        P("rep", "fsdp", None, None, None),
        P("rep", "fsdp", None, None, None),
        P("rep", "fsdp", None),
    )
    return jax.shard_map(
        on_device, mesh=mesh, in_specs=in_specs, out_specs=out_specs, check_vma=False
    )
```
